128 devices in a mesh: ctx: 16 (over y, x), head: 8 (over z, core).
Axes of the slice: x: 4, y: 4, z: 4, core: 2. Of those that a mesh axis runs over, the one named last changes fastest.
Arguments:
- query_input: bfloat16 [16, 1024, 4096], P('ctx', 'head'), may hold values from -6 to 6
- key_input: bfloat16 [16, 1024, 512], P('ctx', 'head'), may hold values from -6 to 6
- value_input: bfloat16 [16, 1024, 512], P('ctx', 'head'), may hold values from -6 to 6
- grad_input: bfloat16 [16, 1024, 4096], P('ctx', 'head'), may hold values from -6 to 6
Outputs:
- attended: bfloat16 [16, 1024, 4096], P('ctx', 'head')
- query_grad: float32 [16, 1024, 4096], P('ctx', 'head')
- key_grad: float32 [16, 1024, 512], P('ctx', 'head')
- value_grad: float32 [16, 1024, 512], P('ctx', 'head')
The draws below stay inside these ranges and needn't reach their ends.
All inputs are finite; a program needn't handle non-finite values.
Results may differ from the reference program's by a relative error of at most 0.0076.
Values may be sent and summed in bfloat16 or wider, within the bound.
No kernel may reach another device: no remote copies, remote signals or barrier semaphores. Data moves between devices by JAX's collectives and lax.ppermute only.
A program may use at most 192 MiB of HBM per device.

```python
import math
import jax
import jax.numpy as jnp
from jax import lax

HD = 128
HEADS = 32
KV_HEADS = 4
STRETCH = 256
BATCH = 4
SEQ = 4096
N_CTX = 16


def block_layout(tensor):
    columns = tensor.shape[-1]
    block_count = SEQ // STRETCH
    return tensor.reshape(BATCH, block_count, STRETCH, columns).transpose(1, 0, 2, 3).reshape(block_count, BATCH * STRETCH, columns)


def draw_query_input(key, part):
    full_shape = (BATCH, SEQ, HEADS, HD)
    base_key = jax.random.fold_in(key, 11)
    sample = jax.random.truncated_normal(base_key, -6.0, 6.0, full_shape, jnp.float32)
    return block_layout(sample.reshape(BATCH, SEQ, HEADS * HD)).astype(jnp.bfloat16)


def draw_key_input(key, part):
    full_shape = (BATCH, SEQ, KV_HEADS, HD)
    base_key = jax.random.fold_in(key, 13)
    sample = jax.random.truncated_normal(base_key, -6.0, 6.0, full_shape, jnp.float32)
    return block_layout(sample.reshape(BATCH, SEQ, KV_HEADS * HD)).astype(jnp.bfloat16)


def block_levels(rng, dims, cuts, low, high):
    level = 1.0
    for dim, parts in cuts:
        steps = jax.random.uniform(jax.random.fold_in(jax.random.fold_in(rng, 6), dim), (parts,), jnp.float32, low / len(cuts), high / len(cuts))
        level = level * jnp.repeat(jnp.exp(steps), dims[dim] // parts).reshape((-1,) + (1,) * (len(dims) - 1 - dim))
    return level


def centred(own_key, extent, spread, most, pieces=(), held_as=jnp.bfloat16):
    drawn = spread * jax.random.normal(own_key, extent, jnp.float32)
    if pieces:
        drawn = drawn * block_levels(own_key, extent, pieces, -0.22, 0.18)
    return jnp.clip(drawn, -most, most).astype(held_as)


def setup_inputs(seed: int = 0) -> dict:
    splits = jax.random.split(jax.random.key(seed), 5)
    return {
        "query_input": draw_query_input(jax.random.fold_in(splits[4], 71), 0),
        "key_input": draw_key_input(jax.random.fold_in(splits[4], 71), 0),
        "value_input": centred(splits[2], (N_CTX, BATCH * STRETCH, KV_HEADS * HD), 1.0, 6.0, ((0, 16), (1, 8))),
        "grad_input": centred(splits[3], (N_CTX, BATCH * STRETCH, HEADS * HD), 1.0, 6.0, ((0, 16), (1, 8))),
    }


def rounded(tensor):
    return lax.optimization_barrier(tensor.astype(jnp.bfloat16)).astype(jnp.float32)

def reference(query_input, key_input, value_input, grad_input):
    sharing = HEADS // KV_HEADS
    scaling = 1.0 / math.sqrt(HD)

    def to_sequences(tensor):
        columns = tensor.shape[-1]
        return tensor.reshape(N_CTX, BATCH, STRETCH, columns).transpose(1, 0, 2, 3).reshape(BATCH, SEQ, columns)

    def to_blocks(tensor):
        columns = tensor.shape[-1]
        return tensor.reshape(BATCH, N_CTX, STRETCH, columns).transpose(1, 0, 2, 3).reshape(N_CTX, BATCH * STRETCH, columns)

    def split_queries(tensor):
        return to_sequences(tensor).reshape(BATCH, SEQ, KV_HEADS, sharing, HD).transpose(0, 2, 3, 1, 4).reshape(BATCH * KV_HEADS, sharing, SEQ, HD)

    def split_pairs(tensor):
        return to_sequences(tensor).reshape(BATCH, SEQ, KV_HEADS, HD).transpose(0, 2, 1, 3).reshape(BATCH * KV_HEADS, SEQ, HD)
    positions = jnp.arange(SEQ, dtype=jnp.int32)
    causal = positions[None, :] <= positions[:, None]

    def single(operands):
        query_part = operands[0].astype(jnp.float32)
        key_part = operands[1].astype(jnp.float32)
        value_part = operands[2].astype(jnp.float32)
        grad_part = operands[3].astype(jnp.float32)
        raw_scores = jnp.einsum('gid,jd->gij', query_part, key_part) * scaling
        scores = jnp.where(causal[None], raw_scores, -jnp.inf)
        highest = lax.optimization_barrier(jnp.max(scores, axis=-1, keepdims=True))
        log_total = highest + jnp.log(lax.optimization_barrier(jnp.sum(jnp.exp(scores - highest), axis=-1, keepdims=True)))
        probs = jnp.exp(scores - log_total)
        weights = rounded(probs)
        attended = jnp.einsum('gij,jd->gid', weights, value_part).astype(jnp.bfloat16)
        attended_back = lax.optimization_barrier(attended).astype(jnp.float32)
        row_dot = lax.optimization_barrier(jnp.sum(grad_part * attended_back, axis=-1, keepdims=True))
        weight_grad = jnp.einsum('gid,jd->gij', grad_part, value_part)
        score_grad = rounded(probs * (weight_grad - row_dot))
        query_grad = scaling * jnp.einsum('gij,jd->gid', score_grad, key_part)
        key_grad = scaling * jnp.einsum('gij,gid->jd', score_grad, query_part)
        value_grad = jnp.einsum('gij,gid->jd', weights, grad_part)
        return (attended, query_grad, key_grad, value_grad)
    attended, query_grad, key_grad, value_grad = lax.map(single, (split_queries(query_input), split_pairs(key_input), split_pairs(value_input), split_queries(grad_input)))

    def merge_queries(tensor):
        return to_blocks(tensor.reshape(BATCH, KV_HEADS, sharing, SEQ, HD).transpose(0, 3, 1, 2, 4).reshape(BATCH, SEQ, HEADS * HD))

    def merge_pairs(tensor):
        return to_blocks(tensor.reshape(BATCH, KV_HEADS, SEQ, HD).transpose(0, 2, 1, 3).reshape(BATCH, SEQ, KV_HEADS * HD))
    return (merge_queries(attended), merge_queries(query_grad), merge_pairs(key_grad), merge_pairs(value_grad))
```

```python
import functools
import math

import jax
import jax.numpy as jnp
from jax import lax
from jax.experimental import pallas as pl
from jax.experimental.pallas import tpu as pltpu
from jax.sharding import PartitionSpec as P

HD = 128
TILE = 256
SHARE = 8
BLOCKS = 16
CHUNKS = 1
BF, F32 = jnp.bfloat16, jnp.float32
SCALE = 1.0 / math.sqrt(HD)
SCALE2 = SCALE * math.log2(math.e)
NT = (((1,), (1,)), ((), ()))
NN = (((1,), (0,)), ((), ()))
AXES = ("ctx", "head")
TEAMS = [
    [c * 8 + 2 * z, c * 8 + 2 * z + 1, (15 - c) * 8 + 2 * z, (15 - c) * 8 + 2 * z + 1]
    for c in range(8)
    for z in range(4)
]
PLANES = [[c * 8 + 2 * z + k for c in range(16) for k in range(2)] for z in range(4)]


def dot(a, b, dims):
    return lax.dot_general(a, b, dims, preferred_element_type=F32)


def causal(width, s, fill):
    row = lax.broadcasted_iota(jnp.int32, (TILE, width), 0)
    col = lax.broadcasted_iota(jnp.int32, (TILE, width), 1) % TILE
    return jnp.where(row <= col, s, fill)


def unpack(g, heads, pieces, q_s, do_s):
    for d in range(4):
        src = g ^ d
        for h in range(heads):
            q_s[src // 2, h, src % 2] = pieces[d][0, :, h * HD : (h + 1) * HD]
            do_s[src // 2, h, src % 2] = pieces[d][1, :, h * HD : (h + 1) * HD]


def value_body(heads, first, last, n_ref, p0, p1, p2, p3, k_ref, *rest):
    if not first:
        prev, *rest = rest
    dv_ref, l_ref, q_s, do_s, dva, e_s, m_s = rest
    width = heads * TILE
    most = jnp.maximum(n_ref[0], n_ref[1])
    unpack(n_ref[2], heads, (p0, p1, p2, p3), q_s, do_s)

    @pl.loop(0, most)
    def _(t):
        dva[t] = jnp.zeros((TILE, HD), F32) if first else prev[t]

    @pl.loop(0, 2)
    def _(it):
        n = n_ref[it]
        qb = q_s[it].reshape(width, HD)
        dob = do_s[it].reshape(width, HD)
        s = causal(width, dot(k_ref[n - 1], qb, NT), -jnp.inf)
        m = jnp.max(s, axis=0, keepdims=True) * SCALE2
        e = jnp.exp2(s * SCALE2 - m)
        l = jnp.sum(e, axis=0, keepdims=True)
        e_s[n - 1] = e.astype(BF)
        m_s[n - 1] = m

        def forward(t, carry):
            m, l = carry
            s = dot(k_ref[t], qb, NT)
            m2 = jnp.maximum(m, jnp.max(s, axis=0, keepdims=True) * SCALE2)
            e = jnp.exp2(s * SCALE2 - m2)
            e_s[t] = e.astype(BF)
            m_s[t] = m2
            return m2, l * jnp.exp2(m - m2) + jnp.sum(e, axis=0, keepdims=True)

        m, l = lax.fori_loop(0, n - 1, forward, (m, l))
        total = m + jnp.log2(l)
        l_ref[it] = total

        def backward(t, _):
            p = e_s[t].astype(F32) * jnp.exp2(m_s[t] - total)
            dva[t] += dot(p.astype(BF), dob, NN)
            return 0

        lax.fori_loop(0, n, backward, 0)

    @pl.loop(0, BLOCKS)
    def _(t):
        @pl.when(t < most)
        def _():
            dv_ref[t] = dva[t].astype(dv_ref.dtype)

        @pl.when(t >= most)
        def _():
            dv_ref[t] = jnp.zeros((TILE, HD), dv_ref.dtype)


def key_body(heads, first, last, n_ref, p0, p1, p2, p3, k_ref, v_ref, l_ref, *rest):
    if not first:
        prev, *rest = rest
    dk_ref, r0, r1, r2, r3, q_s, do_s, o_s, dq_s, kt, vt, dka, p_s, acc = rest
    width = heads * TILE
    g = n_ref[2]
    most = jnp.maximum(n_ref[0], n_ref[1])
    unpack(g, heads, (p0, p1, p2, p3), q_s, do_s)

    @pl.loop(0, most)
    def _(t):
        kt[t] = k_ref[t].T
        vt[t] = v_ref[t].T
        dka[t] = jnp.zeros((TILE, HD), F32) if first else prev[t]

    @pl.loop(0, 2)
    def _(it):
        n = n_ref[it]
        qb = q_s[it].reshape(width, HD)
        dob = do_s[it].reshape(width, HD)
        total = l_ref[it]
        p = causal(width, jnp.exp2(dot(k_ref[n - 1], qb, NT) * SCALE2 - total), 0.0).astype(BF)
        p_s[n - 1] = p
        acc[...] = dot(vt[n - 1], p, NN)

        def forward(t, _):
            p = jnp.exp2(dot(k_ref[t], qb, NT) * SCALE2 - total).astype(BF)
            p_s[t] = p
            acc[...] += dot(vt[t], p, NN)
            return 0

        lax.fori_loop(0, n - 1, forward, 0)
        ot = acc[...].astype(BF)
        row_dot = jnp.sum(dob.T.astype(F32) * ot.astype(F32), axis=0, keepdims=True)
        for h in range(heads):
            for half in range(2):
                at = h * TILE + half * HD
                o_s[it, h, half] = ot[:, at : at + HD].T
        acc[...] = jnp.zeros((HD, width), F32)

        def backward(t, _):
            ds = (p_s[t].astype(F32) * (dot(v_ref[t], dob, NT) - row_dot)).astype(BF)
            dka[t] += dot(ds, qb, NN)
            acc[...] += dot(kt[t], ds, NN)
            return 0

        lax.fori_loop(0, n, backward, 0)
        dqt = (acc[...] * SCALE).astype(BF)
        for h in range(heads):
            for half in range(2):
                at = h * TILE + half * HD
                dq_s[it, h, half] = dqt[:, at : at + HD].T

    for d, out in enumerate((r0, r1, r2, r3)):
        src = g ^ d
        for h in range(heads):
            out[0, :, h * HD : (h + 1) * HD] = o_s[src // 2, h, src % 2]
            out[1, :, h * HD : (h + 1) * HD] = dq_s[src // 2, h, src % 2]

    @pl.loop(0, BLOCKS)
    def _(t):
        @pl.when(t < most)
        def _():
            dk_ref[t] = ((dka[t] * SCALE) if last else dka[t]).astype(dk_ref.dtype)

        @pl.when(t >= most)
        def _():
            dk_ref[t] = jnp.zeros((TILE, HD), dk_ref.dtype)


def assemble_body(chunks, n_ref, *refs):
    pieces, (o_ref, dq_ref) = refs[:-2], refs[-2:]
    g = n_ref[2]
    span = SHARE * HD // chunks
    for c in range(chunks):
        for d in range(4):
            at = pl.multiple_of((g ^ d) * (SHARE * HD) + c * span, span)
            o_ref[0, :, pl.ds(at, span)] = pieces[c * 4 + d][0]
            dq_ref[0, :, pl.ds(at, span)] = pieces[c * 4 + d][1].astype(F32)


VM = pl.BlockSpec(memory_space=pltpu.VMEM)
SM = pl.BlockSpec(memory_space=pltpu.SMEM)


def shape(dims, dtype):
    return jax.ShapeDtypeStruct(dims, dtype)


def value_pass(n, pieces, k, prev, last):
    heads = pieces[0].shape[2] // HD
    width = heads * TILE
    first = prev is None
    held = (2, heads, 2, HD, HD)
    args = (n, *pieces, k) + (() if first else (prev,))
    return pl.pallas_call(
        functools.partial(value_body, heads, first, last),
        out_shape=[shape((BLOCKS, TILE, HD), BF if last else F32), shape((2, 1, width), F32)],
        in_specs=[SM] + [VM] * (len(args) - 1),
        out_specs=[VM] * 2,
        scratch_shapes=[
            pltpu.VMEM(held, BF),
            pltpu.VMEM(held, BF),
            pltpu.VMEM((BLOCKS, TILE, HD), F32),
            pltpu.VMEM((BLOCKS, TILE, width), BF),
            pltpu.VMEM((BLOCKS, 1, width), F32),
        ],
        compiler_params=pltpu.CompilerParams(vmem_limit_bytes=50 * 2**20),
        cost_estimate=pl.CostEstimate(
            flops=17 * 4 * 4 * width * TILE * HD, bytes_accessed=2**22, transcendentals=17 * width * TILE
        ),
        name="value_pass",
    )(*args)


def key_pass(n, pieces, k, v, total, prev, last):
    heads = pieces[0].shape[2] // HD
    width = heads * TILE
    first = prev is None
    held = (2, heads, 2, HD, HD)
    args = (n, *pieces, k, v, total) + (() if first else (prev,))
    return pl.pallas_call(
        functools.partial(key_body, heads, first, last),
        out_shape=[shape((BLOCKS, TILE, HD), BF if last else F32)]
        + [shape((2, HD, heads * HD), BF)] * 4,
        in_specs=[SM] + [VM] * (len(args) - 1),
        out_specs=[VM] * 5,
        scratch_shapes=[pltpu.VMEM(held, BF)] * 4
        + [pltpu.VMEM((BLOCKS, HD, TILE), BF)] * 2
        + [
            pltpu.VMEM((BLOCKS, TILE, HD), F32),
            pltpu.VMEM((BLOCKS, TILE, width), BF),
            pltpu.VMEM((HD, width), F32),
        ],
        compiler_params=pltpu.CompilerParams(vmem_limit_bytes=50 * 2**20),
        cost_estimate=pl.CostEstimate(
            flops=17 * 4 * 10 * width * TILE * HD, bytes_accessed=2**22, transcendentals=17 * width * TILE
        ),
        name="key_pass",
    )(*args)


def assemble(n, pieces, rows):
    return pl.pallas_call(
        functools.partial(assemble_body, len(pieces) // 4),
        out_shape=[shape((1, rows, 4 * SHARE * HD), BF), shape((1, rows, 4 * SHARE * HD), F32)],
        in_specs=[SM] + [VM] * len(pieces),
        out_specs=[VM] * 2,
        compiler_params=pltpu.CompilerParams(vmem_limit_bytes=30 * 2**20),
        name="assemble",
    )(n, *pieces)


def team_swap(pieces):
    out = [pieces[0]]
    for d in (1, 2, 3):
        out.append(lax.ppermute(pieces[d], AXES, [(t[i], t[i ^ d]) for t in TEAMS for i in range(4)]))
    return out


def plane_exchange(x):
    return lax.all_to_all(x, AXES, 0, 0, tiled=True, axis_index_groups=PLANES)


def spread(x, rows):
    heads = x.reshape(rows, 2, 1, 2, HD).transpose(1, 2, 3, 0, 4)
    full = jnp.broadcast_to(heads, (2, 8, 2, rows, HD)).reshape(32, rows, HD)
    return plane_exchange(full).reshape(BLOCKS, TILE, HD)


def collect(x, rows):
    parts = plane_exchange(x.reshape(32, rows, HD)).reshape(2, 8, 2, rows, HD)
    return jnp.sum(parts.astype(F32), axis=1).transpose(2, 0, 1, 3).reshape(1, rows, 4 * HD)


def on_device(query_input, key_input, value_input, grad_input):
    c = lax.axis_index("ctx")
    p = jnp.minimum(c, 15 - c)
    g = 2 * (c >> 3) + (lax.axis_index("head") & 1)
    rows = query_input.shape[1]
    n = jnp.stack([p + 1, 16 - p, g]).astype(jnp.int32)
    span = SHARE * HD // CHUNKS
    q, do = query_input[0], grad_input[0]

    def piece(c, d):
        at = (g ^ d) * (SHARE * HD) + c * span
        return jnp.stack([lax.dynamic_slice_in_dim(x, at, span, 1) for x in (q, do)])

    k = spread(key_input, rows)
    inputs = [team_swap([piece(c, d) for d in range(4)]) for c in range(CHUNKS)]
    v = spread(value_input, rows)
    dv, totals = None, []
    for c in range(CHUNKS):
        dv, total = value_pass(n, inputs[c], k, dv, c == CHUNKS - 1)
        totals.append(total)
    value_grad = collect(dv, rows)
    dk, returned = None, []
    for c in range(CHUNKS):
        dk, *pieces = key_pass(n, inputs[c], k, v, totals[c], dk, c == CHUNKS - 1)
        returned += team_swap(pieces)
    key_grad = collect(dk, rows)
    attended, query_grad = assemble(n, returned, rows)
    return attended, query_grad, key_grad, value_grad


def solution(mesh):
    spec = P("ctx", "head", None)
    return jax.shard_map(
        on_device, mesh=mesh, in_specs=(spec,) * 4, out_specs=(spec,) * 4, check_vma=False
    )
```
